256 devices in a mesh: fsdp: 32 (over y, z_lo, core), tp: 8 (over z_hi, x).
Axes of the slice: x: 4, y: 4, z: 8 (z_hi: 2, z_lo: 4; z = z_hi * 4 + z_lo), core: 2. Of those that a mesh axis runs over, the one named last changes fastest.
Arguments:
- hidden_states: bfloat16 [24576, 8192], P('fsdp', 'tp'), may hold values from -6 to 6
- key_value_weight: bfloat16 [8192, 2048], P('tp'), may hold values from -0.0625 to 0.0625
- doc_lengths: int32 [32, 6], P('fsdp'), may hold values from 1 to 384, 768 in all within a row
- grad_down: float32 [256, 8192, 128], P(('fsdp', 'tp')), may hold values from -6 to 6
- grad_up: float32 [256, 1024, 128], P(('fsdp', 'tp')), may hold values from -6 to 6
- adapter_down: float32 [8, 1024, 128], P('tp', 'fsdp'), may hold values from -0.0625 to 0.0625
- first_down: float32 [8, 1024, 128], P('tp', 'fsdp'), may hold values from -3 to 3
- second_down: float32 [8, 1024, 128], P('tp', 'fsdp'), may hold values from 0.002 to 0.02
- adapter_up: float32 [1024, 128], P(('fsdp', 'tp')), may hold values from -1.5 to 1.5
- first_up: float32 [1024, 128], P(('fsdp', 'tp')), may hold values from -3 to 3
- second_up: float32 [1024, 128], P(('fsdp', 'tp')), may hold values from 0.002 to 0.02
Outputs:
- kv_states: bfloat16 [24576, 2048], P('fsdp', 'tp')
- new_down: float32 [8, 1024, 128], P('tp', 'fsdp')
- new_first_down: float32 [8, 1024, 128], P('tp', 'fsdp')
- new_second_down: float32 [8, 1024, 128], P('tp', 'fsdp')
- new_up: float32 [1024, 128], P(('fsdp', 'tp'))
- new_first_up: float32 [1024, 128], P(('fsdp', 'tp'))
- new_second_up: float32 [1024, 128], P(('fsdp', 'tp'))
The draws below stay inside these ranges and needn't reach their ends.
Inputs may be any that keep to these rules, and one draw needn't show every extreme that they name: `doc_lengths`: each row of 6 lengths sums to 768.
All inputs are finite; a program needn't handle non-finite values.
Results may differ from the reference program's by a relative error of at most 0.018.
Values may be sent and summed in bfloat16 or wider, within the bound.
A program may use at most 64 MiB of HBM per device.

```python
import math
import jax
import jax.numpy as jnp
import numpy as np
from jax import lax

D = 8192
HEAD = 128
R = 64
TOK_DEV = 768
DOCS = 6
KVW = 1024
TOKENS = 24576
TILE_ROWS = 1024
NB = 1024
N_FSDP = 32
N_TP = 8


def strengthened(values, key, source, target, blocks, factor):
    def block_of(dim):
        return (jnp.arange(values.shape[dim]) // (values.shape[dim] // blocks)).reshape((-1,) + (1,) * (values.ndim - 1 - dim))

    one_side = jax.random.permutation(key, blocks)[block_of(target)]
    far = (block_of(target) + blocks // 2) % blocks
    return jnp.where((block_of(source) == one_side) | (block_of(source) == far), factor * values, values)


def shard_levels(rng, shape, shards, low, high):
    loudness = 1.0
    for dim, parts in shards:
        draws = jax.random.uniform(jax.random.fold_in(jax.random.fold_in(rng, 6), dim), (parts,), jnp.float32, low / len(shards), high / len(shards))
        loudness = loudness * jnp.repeat(jnp.exp(draws), shape[dim] // parts).reshape((-1,) + (1,) * (len(shape) - 1 - dim))
    return loudness


def length_profile(amount, total, reach, skew):
    loads = [(1 << 20) // math.isqrt(standing ** skew) + 1 for standing in range(2, amount + 1)]
    spare, counts = total - reach - (amount - 1), [1] * (amount - 1)
    while spare > 0:
        free = [i for i in range(amount - 1) if counts[i] < reach]
        whole, remaining = sum([loads[i] for i in free]), spare
        for i in free:
            addition = min(reach - counts[i], max(1, remaining * loads[i] // whole), spare)
            counts[i] = counts[i] + addition
            spare = spare - addition
    return np.array([reach] + counts)


def ragged_sizes(rng, count, total, limit, skew):
    if count == 2:
        one = jax.random.randint(rng, (), max(1, total - limit), min(limit, total - 1) + 1)
        return jnp.stack([one, total - one])
    sizes = jnp.asarray(length_profile(count, total, limit, skew), jnp.int32)
    twos = (count - 1) // 2
    source_of, taker = sizes[1:1 + 2 * twos:2], sizes[2:2 + 2 * twos:2]
    room = jnp.minimum(source_of - 1, limit - taker)
    moved = jax.random.randint(jax.random.fold_in(rng, 1), (twos,), 0, 1 << 20) % (room + 1)
    sizes = sizes.at[1:1 + 2 * twos:2].set(source_of - moved).at[2:2 + 2 * twos:2].set(taker + moved)
    return sizes[jax.random.permutation(jax.random.fold_in(rng, 2), count)]


def noise(rng, dims, width, most, cuts=(), held_as=jnp.bfloat16):
    array = jax.random.normal(rng, dims, jnp.float32) * width
    if len(cuts) > 0:
        array = shard_levels(rng, dims, cuts, -0.22, 0.18) * array
    return jnp.clip(array, min=-most, max=most).astype(held_as)


def bell_draw_with(own_key, extent, deviation, most, shards, heavy, held_as=jnp.bfloat16):
    array = deviation * jax.random.normal(own_key, extent, jnp.float32)
    if shards:
        array = array * shard_levels(own_key, extent, shards, -0.22, 0.18)
    return jnp.clip(strengthened(array, jax.random.fold_in(own_key, 3), *heavy), -most, most).astype(held_as)


def setup_inputs(seed: int = 0) -> dict:
    key_list = jax.random.split(jax.random.key(seed), 12)
    hidden_states = noise(key_list[0], (TOKENS, D), 1.0, 6.0, ((0, 32), (1, 8)))
    key_value_weight = noise(key_list[1], (D, 2 * KVW), D ** -0.5, 0.0625, ((0, 8),))
    doc_lengths = jax.vmap(lambda own: ragged_sizes(own, DOCS, TOK_DEV, TOK_DEV // 2, 2))(jax.random.split(key_list[2], N_FSDP)).reshape((N_FSDP, DOCS)).astype(jnp.int32)
    grad_down = bell_draw_with(key_list[3], (N_FSDP * N_TP, D, 2 * R), 0.125, 6.0, ((0, 256),), (0, 1, 256, 6.0), jnp.float32)
    grad_up = bell_draw_with(key_list[4], (N_FSDP * N_TP, NB, 128), 0.125, 6.0, ((0, 256),), (0, 1, 256, 6.0), jnp.float32)
    adapter_down = noise(key_list[5], (N_TP, TILE_ROWS, 2 * R), D ** -0.5, 0.0625, ((0, 8), (1, 32)), jnp.float32)
    first_down = noise(key_list[6], (N_TP, TILE_ROWS, 2 * R), 0.2, 3.0, ((0, 8), (1, 32)), jnp.float32)
    second_down = jnp.clip(jnp.exp(math.log(0.02) - 2.30258502 * jax.random.uniform(key_list[7], (N_TP, TILE_ROWS, 2 * R), jnp.float32) ** shard_levels(key_list[7], (N_TP, TILE_ROWS, 2 * R), ((0, 8), (1, 32)), -0.2, 0.2)), 0.002, 0.02)
    adapter_up = noise(key_list[8], (NB, 128), 0.1, 1.5, ((0, 256),), jnp.float32)
    first_up = noise(key_list[9], (NB, 128), 0.2, 3.0, ((0, 256),), jnp.float32)
    second_up = jnp.clip(jnp.exp(math.log(0.02) - 2.30258502 * jax.random.uniform(key_list[10], (NB, 128), jnp.float32) ** shard_levels(key_list[10], (NB, 128), ((0, 256),), -0.2, 0.2)), 0.002, 0.02)
    return {"hidden_states": hidden_states, "key_value_weight": key_value_weight, "doc_lengths": doc_lengths, "grad_down": grad_down, "grad_up": grad_up, "adapter_down": adapter_down, "first_down": first_down, "second_down": second_down, "adapter_up": adapter_up, "first_up": first_up, "second_up": second_up}


beta_one = 0.9
beta_two = 0.999
correct_one = 0.19
correct_two = 0.001999
adam_eps = 1e-08
down_learning_rate = 0.003
rate_up = 0.05
adapter_scale = 2.0
rope_base = 500000.0

def adam_step(current, moment_one, moment_two, gradient, learn_rate):
    moment_one = beta_one * moment_one + (1.0 - beta_one) * gradient
    moment_two = beta_two * moment_two + (1.0 - beta_two) * gradient * gradient
    update = moment_one / correct_one / (jnp.sqrt(moment_two / correct_two) + adam_eps)
    return (current - learn_rate * update, moment_one, moment_two)

def block_adapter(up_rows):
    column = jnp.arange(up_rows.shape[1], dtype=jnp.int32)
    is_value = (column // HEAD % 2).astype(up_rows.dtype)
    key_block = up_rows * (1 - is_value)[None, :]
    value_block = up_rows * is_value[None, :]
    return jnp.concatenate([key_block, value_block], axis=0)

def rotate(summed, lengths):
    token_count = summed.shape[0]
    doc_ends = jnp.cumsum(lengths).astype(jnp.int32)
    token_index = jnp.arange(token_count, dtype=jnp.int32)
    starts = lax.optimization_barrier(jnp.sum(jnp.where(doc_ends[None, :] <= token_index[:, None], lengths[None, :], 0), axis=1)).astype(jnp.int32)
    position = (token_index - starts).astype(jnp.float32)
    frequency = rope_base ** (-(jnp.arange(HEAD // 2, dtype=jnp.float32) * 2.0 / HEAD))
    angles = position[:, None] * frequency[None, :]
    cosine_table = jnp.cos(angles)[:, None, :]
    sine = jnp.sin(angles)[:, None, :]
    head_view = summed.reshape(token_count, -1, 2, HEAD)
    key_part = head_view[:, :, 0]
    value_part = head_view[:, :, 1]
    first_half = key_part[..., :HEAD // 2]
    second_half = key_part[..., HEAD // 2:]
    rotated = jnp.concatenate([first_half * cosine_table - second_half * sine, second_half * cosine_table + first_half * sine], axis=-1)
    return jnp.stack([rotated, value_part], axis=2).reshape(token_count, -1)

def reference(hidden_states, key_value_weight, doc_lengths, grad_down, grad_up, adapter_down, first_down, second_down, adapter_up, first_up, second_up):
    tile_count = adapter_down.shape[0]
    summed_down = lax.optimization_barrier(jnp.sum(grad_down, axis=0)).reshape(adapter_down.shape)
    summed_up = lax.optimization_barrier(jnp.sum(grad_up, axis=0))
    new_down, new_first_down, new_second_down = adam_step(adapter_down, first_down, second_down, summed_down, down_learning_rate)
    new_up, new_first_up, new_second_up = adam_step(adapter_up, first_up, second_up, summed_up, rate_up)
    down_roll = new_down.astype(jnp.bfloat16)
    up_roll = new_up.astype(jnp.bfloat16).reshape(R, 2 * KVW)
    blocked = block_adapter(up_roll)
    weight_tiles = key_value_weight.reshape(tile_count, -1, 2 * KVW)

    def merge_tile(pair):
        down_tile, tile_of_weight = pair
        adapter_delta = jnp.dot(down_tile, blocked, preferred_element_type=jnp.float32)
        return (tile_of_weight.astype(jnp.float32) + adapter_scale * adapter_delta).astype(jnp.bfloat16)
    merged_weight = lax.map(merge_tile, (down_roll, weight_tiles))
    merged_wide = merged_weight.astype(jnp.float32)

    def prefill_group(pair):
        rows_per_group, lengths = pair
        pieces = rows_per_group.astype(jnp.float32).reshape(TOK_DEV, tile_count, -1)
        partial_value = jnp.einsum('tni,nic->ntc', pieces, merged_wide)
        rounded = lax.optimization_barrier(partial_value.astype(jnp.bfloat16))
        summed = lax.optimization_barrier(jnp.sum(rounded.astype(jnp.float32), axis=0))
        return rotate(summed, lengths).astype(jnp.bfloat16)
    states = lax.map(prefill_group, (hidden_states.reshape(N_FSDP, TOK_DEV, D), doc_lengths))
    kv_states = states.reshape(TOKENS, 2 * KVW)
    return (kv_states, new_down, new_first_down, new_second_down, new_up, new_first_up, new_second_up)
```

```python
import jax
import jax.numpy as jnp
from jax import lax
from jax.experimental import pallas as pl
from jax.experimental.pallas import tpu as pltpu
from jax.sharding import PartitionSpec as P

HEAD = 128
TOKENS_LOCAL = 768
FEATURES = 1024
HEAD_COLUMNS = 256
PIECE = 48
MESH = pl.DeviceIdType.MESH

beta_one = 0.9
beta_two = 0.999
correct_one = 0.19
correct_two = 0.001999
adam_eps = 1e-08
down_learning_rate = 0.003
rate_up = 0.05
adapter_scale = 2.0
rope_base = 500000.0

Z_STEPS = (2, 1, 3, 0)
X_STEPS = (2, 1, 3, 0)


def adam_step(current, moment_one, moment_two, gradient, learn_rate):
    moment_one = beta_one * moment_one + (1.0 - beta_one) * gradient
    moment_two = beta_two * moment_two + (1.0 - beta_two) * gradient * gradient
    update = moment_one / correct_one / (jnp.sqrt(moment_two / correct_two) + adam_eps)
    return (current - learn_rate * update, moment_one, moment_two)


def dot(a, b):
    return jnp.dot(a, b, preferred_element_type=jnp.float32)


def kernel(
    hidden, weight, lengths, grad_down, grad_up, p_down, m_down, v_down, p_up, m_up, v_up,
    out, new_p_down, new_m_down, new_v_down, new_p_up, new_m_up, new_v_up,
    hid, wv, gv, cs, cr, ys, yr, zs, zr, ab, hs, hr, hall, xs, xr, own_heads, zbs, zbr,
    table, state, up_state, up_all, new_down_v, new_up_v, out_v,
    ld_sem, core_s, core_r, y_s, y_r, z_s, z_r, a_s, a_r, f_s, f_r, hs_s, hs_r, hg_s, hg_r,
    x_s, x_r, b_s, b_r, u_s, u_r, st_sem, o_sem,
):
    f = lax.axis_index("fsdp")
    t = lax.axis_index("tp")
    y, zl, c, zh, x = f // 8, (f // 2) % 4, f % 2, t // 4, t % 4
    chip = f // 2

    def f_of(y_, zl_, c_):
        return (y_ * 4 + zl_) * 2 + c_

    barrier = pltpu.get_barrier_semaphore()
    partners = [(f_of(y, zl, 1 - c), t)]
    for k in range(1, 16):
        q = (chip + k) % 16
        partners.append((q * 2 + c, t))
    for dz in range(4):
        for k in range(8):
            if k == 0:
                continue
            partners.append((f_of(y, (zl + dz) % 4, c), (t + k) % 8))
    for p in partners:
        pl.semaphore_signal(barrier, inc=1, device_id=p, device_id_type=MESH)

    heads = []
    for half in range(2):
        for dx in X_STEPS:
            zh_ = (1 - zh) if half == 0 else zh
            heads.append((half, dx, zh_ * 4 + (x + dx) % 4))
    loads = {}

    def load(name, src, dst):
        i = len(loads)
        cp = pltpu.make_async_copy(src, dst, ld_sem.at[i])
        cp.start()
        loads[name] = cp

    def load_grad(j):
        z_ = (zl + Z_STEPS[j]) % 4
        load(("d", j), grad_down.at[:, :, z_], gv.at[j, pl.ds(0, 8)])
        load(("u", j), grad_up.at[:, z_], gv.at[j, 8])

    def load_head(i):
        col = pl.multiple_of(heads[i][2] * HEAD_COLUMNS, HEAD_COLUMNS)
        load(("w", i), weight.at[:, pl.ds(col, HEAD_COLUMNS)], wv.at[i])

    load_grad(0)
    load("hid", hidden, hid)
    load_head(0)
    load_grad(1)
    load_head(1)
    load_grad(2)
    load_head(2)
    load_grad(3)
    for i in range(3, 8):
        load_head(i)
    load("p", p_down, state.at[0])
    load("m", m_down, state.at[1])
    load("v", v_down, state.at[2])
    up_state[...] = jnp.zeros_like(up_state)
    load("pu", p_up, up_state.at[pl.ds(0, 4)])
    load("mu", m_up, up_state.at[pl.ds(8, 4)])
    load("vu", v_up, up_state.at[pl.ds(16, 4)])

    copies = []

    def send(src, dst, ss, rs, to):
        cp = pltpu.make_async_remote_copy(
            src_ref=src, dst_ref=dst, send_sem=ss, recv_sem=rs, device_id=to, device_id_type=MESH
        )
        cp.start()
        return cp

    def await_recv(ref, sem):
        pltpu.make_async_copy(ref, ref, sem).wait()

    def phase_a(j):
        loads[("d", j)].wait()
        loads[("u", j)].wait()

        @pl.loop(0, 4)
        def _(k):
            cs[j, k] = gv[j, :, (y + k) % 4, 1 - c].astype(jnp.bfloat16)

        if j == 0:
            pl.semaphore_wait(barrier, len(partners))
        copies.append(send(cs.at[j], cr.at[j], core_s.at[j], core_r.at[j], (f_of(y, zl, 1 - c), t)))

    def phase_b(j):
        await_recv(cr.at[j], core_r.at[j])
        for k in (2, 1, 3):
            ys[j, k - 1] = (
                gv[j, :, (y + k) % 4, c] + cr[j, k].astype(jnp.float32)
            ).astype(jnp.bfloat16)
            copies.append(
                send(
                    ys.at[j, k - 1], yr.at[j, k - 1], y_s.at[j, k - 1], y_r.at[j, k - 1],
                    (f_of((y + k) % 4, zl, c), t),
                )
            )

    rows = lax.broadcasted_iota(jnp.int32, (128, 32), 0)
    cols = lax.broadcasted_iota(jnp.int32, (128, 32), 1)
    tile, r = rows // 16, rows % 16
    wanted = jnp.where(
        r < 4, 4 * tile + r, jnp.where(r < 6, 2 * tile + r - 4, 2 * tile + r + 10)
    )
    pick = jnp.where((wanted == cols) & (r < 8), 1.0, 0.0).astype(jnp.bfloat16)

    def phase_c(j):
        for k in range(3):
            await_recv(yr.at[j, k], y_r.at[j, k])
        total = (
            gv[j, :, y, c]
            + cr[j, 0].astype(jnp.float32)
            + yr[j, 0].astype(jnp.float32)
            + yr[j, 1].astype(jnp.float32)
            + yr[j, 2].astype(jnp.float32)
        ).astype(jnp.bfloat16)
        zs[j, :, 0:32] = total[0:8]
        zs[j, :, 32:48] = dot(pick, total[8]).astype(jnp.bfloat16).reshape(8, 16, 128)
        to_f = f_of(y, (zl + Z_STEPS[j]) % 4, c)
        for k in range(8):
            if Z_STEPS[j] == 0 and k == 0:
                continue
            to_t = (t + k) % 8
            send(zs.at[j, to_t], zr.at[j, k], z_s.at[j], z_r.at[j], (to_f, to_t))

    def up_exchange():
        for name in ("pu", "mu", "vu"):
            loads[name].wait()
        up_all[t] = up_state[...]
        for k in range(1, 8):
            send(up_state, up_all.at[t], u_s, u_r, (f, (t + k) % 8))

    def head(i):
        half, dx, _ = heads[i]
        loads[("w", i)].wait()
        slot = half * 3 + X_STEPS.index(dx)

        @pl.loop(0, 3)
        def _(m):
            part = pl.ds(pl.multiple_of(m * 256, 256), 256)
            value = dot(hid[part, :], wv[i])
            if dx == 0:
                own_heads[half, part, :] = value
            else:
                xs[slot, part, :] = value.astype(jnp.bfloat16)

        if dx != 0:
            copies.append(
                send(xs.at[slot], xr.at[slot], x_s.at[slot], x_r.at[slot], (f, zh * 4 + (x + dx) % 4))
            )

    def head_forward():
        for s in range(3):
            await_recv(xr.at[s], x_r.at[s])

        @pl.loop(0, 6)
        def _(m):
            part = pl.ds(pl.multiple_of(m * 128, 128), 128)
            zbs[part, :] = (
                own_heads[0, part, :]
                + xr[0, part, :].astype(jnp.float32)
                + xr[1, part, :].astype(jnp.float32)
                + xr[2, part, :].astype(jnp.float32)
            ).astype(jnp.bfloat16)

        copies.append(send(zbs, zbr, b_s, b_r, (f, (1 - zh) * 4 + x)))

    def trig():
        lane = lax.broadcasted_iota(jnp.int32, (128, 128), 1)
        freq = jnp.exp(
            (lane % 64).astype(jnp.float32) * (-2.0 / HEAD * 13.122363377404328)
        )
        shift = jnp.where(lane < 64, 0.5 * 3.141592653589793, 0.0)

        @pl.loop(0, 6)
        def _(m):
            index = lax.broadcasted_iota(jnp.int32, (128, 128), 0) + m * 128
            start = jnp.zeros((128, 128), jnp.int32)
            end = jnp.int32(0)
            for d in range(6):
                end = end + lengths[0, d]
                start = start + jnp.where(index >= end, lengths[0, d], 0)
            angle = (index - start).astype(jnp.float32) * freq
            table[pl.ds(pl.multiple_of(m * 128, 128), 128), :] = jnp.sin(angle + shift)

    phase_a(0)
    loads["hid"].wait()
    head(0)
    phase_a(1)
    phase_b(0)
    head(1)
    phase_a(2)
    phase_b(1)
    head(2)
    phase_a(3)
    phase_b(2)
    head(4)
    phase_b(3)
    phase_c(0)
    head(5)
    phase_c(1)
    head(6)
    up_exchange()
    phase_c(2)
    head(3)
    phase_c(3)
    head(7)
    trig()

    for j in range(3):
        await_recv(zr.at[j], z_r.at[j])
    await_recv(zr.at[3, pl.ds(1, 7)], z_r.at[3])
    total = zs[3, t].astype(jnp.float32)
    for j in range(4):
        for k in range(8):
            if j == 3 and k == 0:
                continue
            total = total + zr[j, k].astype(jnp.float32)
    for name in ("p", "m", "v"):
        loads[name].wait()
    new = adam_step(state[0], state[1], state[2], total[0:32], down_learning_rate)
    ab[chip, c, 0:32] = new[0].astype(jnp.bfloat16)
    await_recv(up_all.at[pl.ds(0, 7)], u_r)
    first, second = up_all[t // 2], up_all[4 + t // 2]
    odd = t % 2 == 1

    def of_head(row):
        return jnp.concatenate(
            [
                jnp.where(odd, first[row + 2 : row + 4], first[row : row + 2]),
                jnp.where(odd, second[row + 2 : row + 4], second[row : row + 2]),
            ],
            axis=0,
        )

    new_head = adam_step(of_head(0), of_head(8), of_head(16), total[36:40], rate_up)[0]
    ab[chip, c, 32:48] = jnp.concatenate(
        [new_head, jnp.zeros((12, 128), jnp.float32)], axis=0
    ).astype(jnp.bfloat16)
    for k in range(1, 16):
        q = (chip + k) % 16
        send(ab.at[chip, c], ab.at[chip, c], a_s, a_r, (q * 2 + c, t))
    new_up = adam_step(
        up_state[0:4], up_state[8:12], up_state[16:20], total[32:36], rate_up
    )
    outs = []
    for n, ref in enumerate((new_p_down, new_m_down, new_v_down)):
        new_down_v[n] = new[n]
        outs.append(pltpu.make_async_copy(new_down_v.at[n], ref, o_sem.at[n]))
    for n, ref in enumerate((new_p_up, new_m_up, new_v_up)):
        new_up_v[n] = new_up[n]
        outs.append(pltpu.make_async_copy(new_up_v.at[n], ref, o_sem.at[3 + n]))
    for cp in outs:
        cp.start()

    await_recv(ab.at[pl.ds(0, 15), c], a_r)
    copies.append(send(ab.at[:, c], ab.at[:, c], f_s, f_r, (f_of(y, zl, 1 - c), t)))
    head_forward()
    await_recv(ab.at[:, 1 - c], f_r)

    adapter = ab[:, :, 0:32].reshape(FEATURES, 128)
    for k in (4, 5, 3, 6, 2, 7, 1, 0):
        to_t = (t + k) % 8
        part = pl.ds(pl.multiple_of(to_t * 96, 96), 96)
        hs[to_t] = dot(hid[part, :], adapter).astype(jnp.bfloat16)
        if k:
            send(hs.at[to_t], hr.at[k - 1], hs_s, hs_r, (f, to_t))
    select_row = lax.broadcasted_iota(jnp.int32, (128, 512), 0)
    select_col = lax.broadcasted_iota(jnp.int32, (128, 512), 1)
    place = (select_row % 64) // 2 * 16 + select_row % 2 * 2
    key_pick = jnp.where((select_row < 64) & (select_col == place), 1.0, 0.0)
    value_pick = jnp.where((select_row >= 64) & (select_col == place + 1), 1.0, 0.0)
    rolls = ab[:, :, 32:48].reshape(512, 128)
    key_block = dot(key_pick.astype(jnp.bfloat16), rolls).astype(jnp.bfloat16)
    value_block = dot(value_pick.astype(jnp.bfloat16), rolls).astype(jnp.bfloat16)

    await_recv(hr, hs_r)
    mixed = hs[t].astype(jnp.float32)
    for k in range(7):
        mixed = mixed + hr[k].astype(jnp.float32)
    hall[t] = mixed.astype(jnp.bfloat16)
    for k in (4, 5, 3, 6, 2, 7, 1):
        send(hall.at[t], hall.at[t], hg_s, hg_r, (f, (t + k) % 8))

    for s in range(3, 6):
        await_recv(xr.at[s], x_r.at[s])
    await_recv(zbr, b_r)

    @pl.loop(0, 6)
    def _(m):
        part = pl.ds(pl.multiple_of(m * 128, 128), 128)
        own_heads[1, part, :] = (
            own_heads[1, part, :]
            + xr[3, part, :].astype(jnp.float32)
            + xr[4, part, :].astype(jnp.float32)
            + xr[5, part, :].astype(jnp.float32)
            + zbr[part, :].astype(jnp.float32)
        )

    await_recv(hall.at[pl.ds(0, 7)], hg_r)
    final = []
    low = lax.broadcasted_iota(jnp.int32, (96, 128), 1) < 64
    for m in range(8):
        part = pl.ds(m * 96, 96)
        rot = table[part, :]
        swapped = pltpu.roll(rot, 64, 1)
        cosine = jnp.where(low, rot, swapped)
        sine = jnp.where(low, -swapped, rot)
        key = own_heads[1, part, 0:128] + adapter_scale * dot(hall[m], key_block)
        value = own_heads[1, part, 128:256] + adapter_scale * dot(hall[m], value_block)
        out_v[part, 0:128] = (key * cosine + pltpu.roll(key, 64, 1) * sine).astype(jnp.bfloat16)
        out_v[part, 128:256] = value.astype(jnp.bfloat16)
    last = pltpu.make_async_copy(out_v, out, st_sem)
    last.start()

    for cp in copies:
        cp.wait_send()
    for j in range(3):
        await_recv(zs.at[j], z_s.at[j])
    await_recv(zs.at[3, pl.ds(1, 7)], z_s.at[3])
    await_recv(up_all.at[pl.ds(0, 7)], u_s)
    await_recv(ab.at[pl.ds(0, 15), c], a_s)
    await_recv(hr, hs_s)
    await_recv(hr, hg_s)
    for cp in outs:
        cp.wait()
    last.wait()


def on_device(
    hidden_states, key_value_weight, doc_lengths, grad_down, grad_up,
    adapter_down, first_down, second_down, adapter_up, first_up, second_up,
):
    bf16, f32 = jnp.bfloat16, jnp.float32
    anywhere = pl.BlockSpec(memory_space=pl.ANY)
    vm = pltpu.VMEM
    dma = pltpu.SemaphoreType.DMA
    results = pl.pallas_call(
        kernel,
        out_shape=[jax.ShapeDtypeStruct((TOKENS_LOCAL, HEAD_COLUMNS), bf16)]
        + [jax.ShapeDtypeStruct((32, 128), f32)] * 3
        + [jax.ShapeDtypeStruct((4, 128), f32)] * 3,
        in_specs=[anywhere, anywhere, pl.BlockSpec(memory_space=pltpu.SMEM)] + [anywhere] * 8,
        out_specs=[anywhere] * 7,
        scratch_shapes=[
            vm((TOKENS_LOCAL, FEATURES), bf16),
            vm((8, FEATURES, HEAD_COLUMNS), bf16),
            vm((4, 9, 4, 2, 32, 128), f32),
            vm((4, 4, 9, 32, 128), bf16),
            vm((4, 4, 9, 32, 128), bf16),
            vm((4, 3, 9, 32, 128), bf16),
            vm((4, 3, 9, 32, 128), bf16),
            vm((4, 8, PIECE, 128), bf16),
            vm((4, 8, PIECE, 128), bf16),
            vm((16, 2, PIECE, 128), bf16),
            vm((8, 96, 128), bf16),
            vm((7, 96, 128), bf16),
            vm((8, 96, 128), bf16),
            vm((6, TOKENS_LOCAL, HEAD_COLUMNS), bf16),
            vm((6, TOKENS_LOCAL, HEAD_COLUMNS), bf16),
            vm((2, TOKENS_LOCAL, HEAD_COLUMNS), f32),
            vm((TOKENS_LOCAL, HEAD_COLUMNS), bf16),
            vm((TOKENS_LOCAL, HEAD_COLUMNS), bf16),
            vm((TOKENS_LOCAL, 128), f32),
            vm((3, 32, 128), f32),
            vm((24, 128), f32),
            vm((8, 24, 128), f32),
            vm((3, 32, 128), f32),
            vm((3, 4, 128), f32),
            vm((TOKENS_LOCAL, HEAD_COLUMNS), bf16),
            dma((24,)),
            dma((4,)), dma((4,)),
            dma((4, 3)), dma((4, 3)),
            dma((4,)), dma((4,)),
            dma(()), dma(()),
            dma(()), dma(()),
            dma(()), dma(()),
            dma(()), dma(()),
            dma((6,)), dma((6,)),
            dma(()), dma(()),
            dma(()), dma(()),
            dma(()),
            dma((6,)),
        ],
        compiler_params=pltpu.CompilerParams(
            collective_id=0, has_side_effects=True, vmem_limit_bytes=56 * 1024 * 1024
        ),
        cost_estimate=pl.CostEstimate(
            flops=2 * TOKENS_LOCAL * FEATURES * 2200, bytes_accessed=12 << 20, transcendentals=0
        ),
    )(
        hidden_states,
        key_value_weight,
        doc_lengths,
        grad_down.reshape(8, 4, 4, 2, 32, 128),
        grad_up.reshape(4, 4, 2, 32, 128),
        adapter_down[0],
        first_down[0],
        second_down[0],
        adapter_up,
        first_up,
        second_up,
    )
    states, p_down, m_down, v_down, p_up, m_up, v_up = results
    return (states, p_down[None], m_down[None], v_down[None], p_up, m_up, v_up)


def solution(mesh):
    matrix = P(("fsdp", "tp"), None)
    down = P("tp", "fsdp", None)
    partial = P(("fsdp", "tp"), None, None)
    in_specs = (
        P("fsdp", "tp"), P("tp", None), P("fsdp", None), partial, partial,
        down, down, down, matrix, matrix, matrix,
    )
    out_specs = (P("fsdp", "tp"), down, down, down, matrix, matrix, matrix)
    return jax.shard_map(
        on_device, mesh=mesh, in_specs=in_specs, out_specs=out_specs, check_vma=False
    )
```

```python
import jax
import jax.numpy as jnp
from jax import lax
from jax.experimental import pallas as pl
from jax.experimental.pallas import tpu as pltpu
from jax.sharding import PartitionSpec as P

HEAD = 128
TOKENS_LOCAL = 768
FEATURES = 1024
HEAD_COLUMNS = 256
PIECE = 48
MESH = pl.DeviceIdType.MESH

beta_one = 0.9
beta_two = 0.999
correct_one = 0.19
correct_two = 0.001999
adam_eps = 1e-08
down_learning_rate = 0.003
rate_up = 0.05
adapter_scale = 2.0
rope_base = 500000.0

Z_STEPS = (2, 1, 3, 0)
X_STEPS = (2, 1, 3, 0)


def adam_step(current, moment_one, moment_two, gradient, learn_rate):
    moment_one = beta_one * moment_one + (1.0 - beta_one) * gradient
    moment_two = beta_two * moment_two + (1.0 - beta_two) * gradient * gradient
    update = moment_one / correct_one / (jnp.sqrt(moment_two / correct_two) + adam_eps)
    return (current - learn_rate * update, moment_one, moment_two)


def dot(a, b):
    return jnp.dot(a, b, preferred_element_type=jnp.float32)


def kernel(
    hidden, weight, lengths, grad_down, grad_up, p_down, m_down, v_down, p_up, m_up, v_up,
    out_h, new_down_h, new_up_h,
    hid, wv, gv, cs, cr, ys, yr, zs, zr, ab, hs, hr, hall, far, mid, near, near_b, xr, own_heads, zbs, zbr,
    table, state, up_state, up_all, out_v, new_down_v, new_up_v,
    ld_sem, core_s, core_r, y_s, y_r, z_s, z_r, a_s, a_r, f_s, f_r, hs_s, hs_r, hg_s, hg_r,
    far_s, far_r, x_s, x_r, b_s, b_r, u_s, u_r, o_sem,
):
    f = lax.axis_index("fsdp")
    t = lax.axis_index("tp")
    y, zl, c, zh, x = f // 8, (f // 2) % 4, f % 2, t // 4, t % 4
    chip = f // 2

    def f_of(y_, zl_, c_):
        return (y_ * 4 + zl_) * 2 + c_

    barrier = pltpu.get_barrier_semaphore()
    partners = [(f_of(y, zl, 1 - c), t)]
    for k in range(1, 16):
        q = (chip + k) % 16
        partners.append((q * 2 + c, t))
    for dz in range(4):
        for k in range(8):
            if k == 0:
                continue
            partners.append((f_of(y, (zl + dz) % 4, c), (t + k) % 8))
    for p in partners:
        pl.semaphore_signal(barrier, inc=1, device_id=p, device_id_type=MESH)

    heads = []
    for half in range(2):
        for dx in X_STEPS:
            zh_ = (1 - zh) if half == 0 else zh
            heads.append((half, dx, zh_ * 4 + (x + dx) % 4))
    loads = {}

    def load(name, src, dst):
        i = len(loads)
        cp = pltpu.make_async_copy(src, dst, ld_sem.at[i])
        cp.start()
        loads[name] = cp

    def load_grad(j):
        z_ = (zl + Z_STEPS[j]) % 4
        load(("d", j), grad_down.at[:, :, z_], gv.at[j, pl.ds(0, 8)])
        load(("u", j), grad_up.at[:, z_], gv.at[j, 8])

    def load_head(i):
        col = pl.multiple_of(heads[i][2] * HEAD_COLUMNS, HEAD_COLUMNS)
        load(("w", i), weight.at[:, pl.ds(col, HEAD_COLUMNS)], wv.at[i])

    load_grad(0)
    load_grad(1)
    load("hid", hidden, hid)
    load_head(0)
    load_grad(2)
    load_grad(3)
    for i in range(1, 8):
        load_head(i)
    load("p", p_down, state.at[0])
    load("m", m_down, state.at[1])
    load("v", v_down, state.at[2])
    up_state[...] = jnp.zeros_like(up_state)
    load("pu", p_up, up_state.at[pl.ds(0, 4)])
    load("mu", m_up, up_state.at[pl.ds(8, 4)])
    load("vu", v_up, up_state.at[pl.ds(16, 4)])

    def send(src, dst, ss, rs, to):
        pltpu.make_async_remote_copy(
            src_ref=src, dst_ref=dst, send_sem=ss, recv_sem=rs, device_id=to, device_id_type=MESH
        ).start()

    def await_bytes(ref, sem):
        pltpu.make_async_copy(ref, ref, sem).wait()

    sent = []

    def phase_a(j):
        loads[("d", j)].wait()
        loads[("u", j)].wait()

        @pl.loop(0, 4)
        def _(k):
            cs[j, k] = gv[j, :, (y + k) % 4, 1 - c].astype(jnp.bfloat16)

    def core_send(j):
        send(cs.at[j], cr.at[j], core_s.at[j], core_r.at[j], (f_of(y, zl, 1 - c), t))
        sent.append((cs.at[j], core_s.at[j]))

    def phase_b(j):
        await_bytes(cr.at[j], core_r.at[j])
        for k in (2, 1, 3):
            ys[j, k - 1] = (
                gv[j, :, (y + k) % 4, c] + cr[j, k].astype(jnp.float32)
            ).astype(jnp.bfloat16)
            send(
                ys.at[j, k - 1], yr.at[j, k - 1], y_s.at[j, k - 1], y_r.at[j, k - 1],
                (f_of((y + k) % 4, zl, c), t),
            )
            sent.append((ys.at[j, k - 1], y_s.at[j, k - 1]))

    rows = lax.broadcasted_iota(jnp.int32, (128, 32), 0)
    cols = lax.broadcasted_iota(jnp.int32, (128, 32), 1)
    tile, r = rows // 16, rows % 16
    wanted = jnp.where(
        r < 4, 4 * tile + r, jnp.where(r < 6, 2 * tile + r - 4, 2 * tile + r + 10)
    )
    pick = jnp.where((wanted == cols) & (r < 8), 1.0, 0.0).astype(jnp.bfloat16)

    def phase_c(j):
        for k in range(3):
            await_bytes(yr.at[j, k], y_r.at[j, k])
        total = (
            gv[j, :, y, c]
            + cr[j, 0].astype(jnp.float32)
            + yr[j, 0].astype(jnp.float32)
            + yr[j, 1].astype(jnp.float32)
            + yr[j, 2].astype(jnp.float32)
        ).astype(jnp.bfloat16)
        zs[j, :, 0:32] = total[0:8]
        zs[j, :, 32:48] = dot(pick, total[8]).astype(jnp.bfloat16).reshape(8, 16, 128)
        to_f = f_of(y, (zl + Z_STEPS[j]) % 4, c)
        for k in range(8):
            if Z_STEPS[j] == 0 and k == 0:
                continue
            to_t = (t + k) % 8
            send(zs.at[j, to_t], zr.at[j, k], z_s.at[j], z_r.at[j], (to_f, to_t))
        sent.append((zs.at[j] if Z_STEPS[j] else zs.at[j, pl.ds(1, 7)], z_s.at[j]))

    def up_exchange():
        for name in ("pu", "mu", "vu"):
            loads[name].wait()
        up_all[t] = up_state[...]
        for k in range(1, 8):
            send(up_state, up_all.at[t], u_s, u_r, (f, (t + k) % 8))
        sent.append((up_all.at[pl.ds(0, 7)], u_s))

    upper, lower = pl.ds(0, 384), pl.ds(384, 384)
    x_next, x_prev = (f, zh * 4 + (x + 1) % 4), (f, zh * 4 + (x + 3) % 4)

    def product(i, place):
        loads[("w", i)].wait()

        @pl.loop(0, 3)
        def _(m):
            part = pl.ds(pl.multiple_of(m * 256, 256), 256)
            place[part, :] = dot(hid[part, :], wv[i]).astype(place.dtype)

    def far_head(half):
        product(half * 4, far.at[half])

    def far_send(half):
        send(far.at[half, upper], mid.at[half, 0], far_s.at[half, 0], far_r.at[half, 0], x_next)
        send(far.at[half, lower], mid.at[half, 1], far_s.at[half, 1], far_r.at[half, 1], x_prev)
        sent.append((far.at[half, upper], far_s.at[half, 0]))
        sent.append((far.at[half, lower], far_s.at[half, 1]))

    def near_head(half, side):
        product(half * 4 + 1 + side, near.at[side])
        mine = lower if side == 0 else upper

        @pl.loop(0, 3)
        def _(m):
            part = pl.ds(pl.multiple_of((384 if side == 0 else 0) + m * 128, 128), 128)
            near_b[half, side, part, :] = near[side, part, :].astype(jnp.bfloat16)

        send(
            near_b.at[half, side, mine], xr.at[half, side, mine], x_s.at[half, side, 0], x_r.at[half, side, 0],
            x_next if side == 0 else x_prev,
        )
        sent.append((near_b.at[half, side, mine], x_s.at[half, side, 0]))

    def near_sum(half, side):
        await_bytes(mid.at[half, side], far_r.at[half, side])
        mine = upper if side == 0 else lower

        @pl.loop(0, 3)
        def _(m):
            local = pl.ds(pl.multiple_of(m * 128, 128), 128)
            part = pl.ds(pl.multiple_of((0 if side == 0 else 384) + m * 128, 128), 128)
            near_b[half, side, part, :] = (
                near[side, part, :] + mid[half, side, local, :].astype(jnp.float32)
            ).astype(jnp.bfloat16)

        send(
            near_b.at[half, side, mine], xr.at[half, side, mine], x_s.at[half, side, 1], x_r.at[half, side, 1],
            x_next if side == 0 else x_prev,
        )
        sent.append((near_b.at[half, side, mine], x_s.at[half, side, 1]))

    def own_head(half):
        product(half * 4 + 3, own_heads.at[half])

    def head_arrive(half):
        for side in range(2):
            await_bytes(xr.at[half, side, lower], x_r.at[half, side, 0])
            await_bytes(xr.at[half, side, upper], x_r.at[half, side, 1])

    def head_forward():
        head_arrive(0)

        @pl.loop(0, 6)
        def _(m):
            part = pl.ds(pl.multiple_of(m * 128, 128), 128)
            zbs[part, :] = (
                own_heads[0, part, :]
                + xr[0, 0, part, :].astype(jnp.float32)
                + xr[0, 1, part, :].astype(jnp.float32)
            ).astype(jnp.bfloat16)

        send(zbs, zbr, b_s, b_r, (f, (1 - zh) * 4 + x))
        sent.append((zbs, b_s))

    def trig():
        lane = lax.broadcasted_iota(jnp.int32, (128, 128), 1)
        freq = jnp.exp(
            (lane % 64).astype(jnp.float32) * (-2.0 / HEAD * 13.122363377404328)
        )
        shift = jnp.where(lane < 64, 0.5 * 3.141592653589793, 0.0)

        @pl.loop(0, 6)
        def _(m):
            index = lax.broadcasted_iota(jnp.int32, (128, 128), 0) + m * 128
            start = jnp.zeros((128, 128), jnp.int32)
            end = jnp.int32(0)
            for d in range(6):
                end = end + lengths[0, d]
                start = start + jnp.where(index >= end, lengths[0, d], 0)
            angle = (index - start).astype(jnp.float32) * freq
            table[pl.ds(pl.multiple_of(m * 128, 128), 128), :] = jnp.sin(angle + shift)

    phase_a(0)
    phase_a(1)
    loads["hid"].wait()
    far_head(0)
    phase_a(2)
    phase_a(3)
    pl.semaphore_wait(barrier, len(partners))
    for j in range(4):
        core_send(j)
    far_send(0)
    phase_b(0)
    near_head(0, 0)
    phase_b(1)
    near_head(0, 1)
    phase_b(2)
    phase_b(3)
    up_exchange()
    near_sum(0, 0)
    near_sum(0, 1)
    phase_c(0)
    own_head(0)
    phase_c(1)
    far_head(1)
    phase_c(2)
    phase_c(3)
    far_send(1)
    near_head(1, 0)
    near_head(1, 1)
    own_head(1)
    trig()
    select_row = lax.broadcasted_iota(jnp.int32, (128, 512), 0)
    select_col = lax.broadcasted_iota(jnp.int32, (128, 512), 1)
    place = (select_row % 64) // 2 * 16 + select_row % 2 * 2
    key_pick = jnp.where((select_row < 64) & (select_col == place), 1.0, 0.0)
    value_pick = jnp.where((select_row >= 64) & (select_col == place + 1), 1.0, 0.0)
    for j in range(3):
        await_bytes(zr.at[j], z_r.at[j])
    await_bytes(zr.at[3, pl.ds(1, 7)], z_r.at[3])
    total = zs[3, t].astype(jnp.float32)
    for j in range(4):
        for k in range(8):
            if j == 3 and k == 0:
                continue
            total = total + zr[j, k].astype(jnp.float32)
    for name in ("p", "m", "v"):
        loads[name].wait()
    new = adam_step(state[0], state[1], state[2], total[0:32], down_learning_rate)
    ab[chip, c, 0:32] = new[0].astype(jnp.bfloat16)
    await_bytes(up_all.at[pl.ds(0, 7)], u_r)
    first, second = up_all[t // 2], up_all[4 + t // 2]
    odd = t % 2 == 1

    def of_head(row):
        return jnp.concatenate(
            [
                jnp.where(odd, first[row + 2 : row + 4], first[row : row + 2]),
                jnp.where(odd, second[row + 2 : row + 4], second[row : row + 2]),
            ],
            axis=0,
        )

    new_head = adam_step(of_head(0), of_head(8), of_head(16), total[36:40], rate_up)[0]
    ab[chip, c, 32:48] = jnp.concatenate(
        [new_head, jnp.zeros((12, 128), jnp.float32)], axis=0
    ).astype(jnp.bfloat16)
    for k in range(1, 16):
        q = (chip + k) % 16
        send(ab.at[chip, c], ab.at[chip, c], a_s, a_r, (q * 2 + c, t))
    sent.append((ab.at[pl.ds(0, 15), c], a_s))
    new_up = adam_step(
        up_state[0:4], up_state[8:12], up_state[16:20], total[32:36], rate_up
    )
    for n in range(3):
        new_down_v[n] = new[n]
        new_up_v[n] = jnp.concatenate([new_up[n], new_up[n]], axis=0)
    outs = [
        pltpu.make_async_copy(new_down_v, new_down_h, o_sem.at[0]),
        pltpu.make_async_copy(new_up_v, new_up_h, o_sem.at[1]),
    ]
    for move in outs:
        move.start()

    near_sum(1, 0)
    near_sum(1, 1)
    await_bytes(ab.at[pl.ds(0, 15), c], a_r)
    send(ab.at[:, c], ab.at[:, c], f_s, f_r, (f_of(y, zl, 1 - c), t))
    sent.append((ab.at[:, c], f_s))
    head_forward()
    await_bytes(ab.at[:, 1 - c], f_r)

    adapter = ab[:, :, 0:32].reshape(FEATURES, 128)
    for m in range(2):
        part = pl.ds(m * 384, 384)
        hs[m * 4 : m * 4 + 4] = dot(hid[part, :], adapter).astype(jnp.bfloat16).reshape(4, 96, 128)
    for k in (4, 5, 3, 6, 2, 7, 1):
        to_t = (t + k) % 8
        send(hs.at[to_t], hr.at[k - 1], hs_s, hs_r, (f, to_t))
    sent.append((hr, hs_s))
    rolls = ab[:, :, 32:48].reshape(512, 128)
    key_block = dot(key_pick.astype(jnp.bfloat16), rolls).astype(jnp.bfloat16)
    value_block = dot(value_pick.astype(jnp.bfloat16), rolls).astype(jnp.bfloat16)

    await_bytes(hr, hs_r)
    mixed = hs[t].astype(jnp.float32)
    for k in range(7):
        mixed = mixed + hr[k].astype(jnp.float32)
    hall[t] = mixed.astype(jnp.bfloat16)
    for k in (4, 5, 3, 6, 2, 7, 1):
        send(hall.at[t], hall.at[t], hg_s, hg_r, (f, (t + k) % 8))
    sent.append((hr, hg_s))

    head_arrive(1)
    await_bytes(zbr, b_r)

    @pl.loop(0, 6)
    def _(m):
        part = pl.ds(pl.multiple_of(m * 128, 128), 128)
        own_heads[1, part, :] = (
            own_heads[1, part, :]
            + xr[1, 0, part, :].astype(jnp.float32)
            + xr[1, 1, part, :].astype(jnp.float32)
            + zbr[part, :].astype(jnp.float32)
        )

    await_bytes(hall.at[pl.ds(0, 7)], hg_r)
    low = lax.broadcasted_iota(jnp.int32, (96, 128), 1) < 64
    for m in range(8):
        part = pl.ds(m * 96, 96)
        if m == 4:
            half_rows = pl.ds(0, 384)
            outs.append(pltpu.make_async_copy(out_v.at[half_rows], out_h.at[half_rows], o_sem.at[2]))
            outs[-1].start()
        rot = table[part, :]
        swapped = pltpu.roll(rot, 64, 1)
        cosine = jnp.where(low, rot, swapped)
        sine = jnp.where(low, -swapped, rot)
        key = own_heads[1, part, 0:128] + adapter_scale * dot(hall[m], key_block)
        value = own_heads[1, part, 128:256] + adapter_scale * dot(hall[m], value_block)
        out_v[part, 0:128] = (key * cosine + pltpu.roll(key, 64, 1) * sine).astype(jnp.bfloat16)
        out_v[part, 128:256] = value.astype(jnp.bfloat16)

    half_rows = pl.ds(384, 384)
    outs.append(pltpu.make_async_copy(out_v.at[half_rows], out_h.at[half_rows], o_sem.at[3]))
    outs[-1].start()

    for ref, sem in sent:
        await_bytes(ref, sem)
    for move in outs:
        move.wait()


def write_out(states, down, up, *refs):
    outs, sem = refs[:7], refs[7]
    parts = [states] + [down.at[n] for n in range(3)] + [up.at[n, pl.ds(0, 4)] for n in range(3)]
    moves = [pltpu.make_async_copy(a, b, sem.at[n]) for n, (a, b) in enumerate(zip(parts, outs))]
    for move in moves:
        move.start()
    for move in moves:
        move.wait()


def on_device(
    hidden_states, key_value_weight, doc_lengths, grad_down, grad_up,
    adapter_down, first_down, second_down, adapter_up, first_up, second_up,
):
    bf16, f32 = jnp.bfloat16, jnp.float32
    anywhere = pl.BlockSpec(memory_space=pl.ANY)
    vm = pltpu.VMEM
    dma = pltpu.SemaphoreType.DMA
    results = pl.pallas_call(
        kernel,
        out_shape=[
            jax.ShapeDtypeStruct((TOKENS_LOCAL, HEAD_COLUMNS), bf16),
            jax.ShapeDtypeStruct((3, 32, 128), f32),
            jax.ShapeDtypeStruct((3, 8, 128), f32),
        ],
        in_specs=[anywhere, anywhere, pl.BlockSpec(memory_space=pltpu.SMEM)] + [anywhere] * 8,
        out_specs=[anywhere] * 3,
        scratch_shapes=[
            vm((TOKENS_LOCAL, FEATURES), bf16),
            vm((8, FEATURES, HEAD_COLUMNS), bf16),
            vm((4, 9, 4, 2, 32, 128), f32),
            vm((4, 4, 9, 32, 128), bf16),
            vm((4, 4, 9, 32, 128), bf16),
            vm((4, 3, 9, 32, 128), bf16),
            vm((4, 3, 9, 32, 128), bf16),
            vm((4, 8, PIECE, 128), bf16),
            vm((4, 8, PIECE, 128), bf16),
            vm((16, 2, PIECE, 128), bf16),
            vm((8, 96, 128), bf16),
            vm((7, 96, 128), bf16),
            vm((8, 96, 128), bf16),
            vm((2, TOKENS_LOCAL, HEAD_COLUMNS), bf16),
            vm((2, 2, TOKENS_LOCAL // 2, HEAD_COLUMNS), bf16),
            vm((2, TOKENS_LOCAL, HEAD_COLUMNS), f32),
            vm((2, 2, TOKENS_LOCAL, HEAD_COLUMNS), bf16),
            vm((2, 2, TOKENS_LOCAL, HEAD_COLUMNS), bf16),
            vm((2, TOKENS_LOCAL, HEAD_COLUMNS), f32),
            vm((TOKENS_LOCAL, HEAD_COLUMNS), bf16),
            vm((TOKENS_LOCAL, HEAD_COLUMNS), bf16),
            vm((TOKENS_LOCAL, 128), f32),
            vm((3, 32, 128), f32),
            vm((24, 128), f32),
            vm((8, 24, 128), f32),
            vm((TOKENS_LOCAL, HEAD_COLUMNS), bf16),
            vm((3, 32, 128), f32),
            vm((3, 8, 128), f32),
            dma((24,)),
            dma((4,)), dma((4,)),
            dma((4, 3)), dma((4, 3)),
            dma((4,)), dma((4,)),
            dma(()), dma(()),
            dma(()), dma(()),
            dma(()), dma(()),
            dma(()), dma(()),
            dma((2, 2)), dma((2, 2)),
            dma((2, 2, 2)), dma((2, 2, 2)),
            dma(()), dma(()),
            dma(()), dma(()),
            dma((4,)),
        ],
        compiler_params=pltpu.CompilerParams(
            collective_id=0, has_side_effects=True, vmem_limit_bytes=56 * 1024 * 1024
        ),
        cost_estimate=pl.CostEstimate(
            flops=2 * TOKENS_LOCAL * FEATURES * 2200, bytes_accessed=12 << 20, transcendentals=0
        ),
    )(
        hidden_states,
        key_value_weight,
        doc_lengths,
        grad_down.reshape(8, 4, 4, 2, 32, 128),
        grad_up.reshape(4, 4, 2, 32, 128),
        adapter_down[0],
        first_down[0],
        second_down[0],
        adapter_up,
        first_up,
        second_up,
    )
    states, p_down, m_down, v_down, p_up, m_up, v_up = pl.pallas_call(
        write_out,
        out_shape=[jax.ShapeDtypeStruct((TOKENS_LOCAL, HEAD_COLUMNS), bf16)]
        + [jax.ShapeDtypeStruct((32, 128), f32)] * 3
        + [jax.ShapeDtypeStruct((4, 128), f32)] * 3,
        in_specs=[pl.BlockSpec(memory_space=vm)] * 3,
        out_specs=[anywhere] * 7,
        scratch_shapes=[dma((7,))],
    )(*results)
    return (states, p_down[None], m_down[None], v_down[None], p_up, m_up, v_up)


def solution(mesh):
    matrix = P(("fsdp", "tp"), None)
    down = P("tp", "fsdp", None)
    partial = P(("fsdp", "tp"), None, None)
    in_specs = (
        P("fsdp", "tp"), P("tp", None), P("fsdp", None), partial, partial,
        down, down, down, matrix, matrix, matrix,
    )
    out_specs = (P("fsdp", "tp"), down, down, down, matrix, matrix, matrix)
    return jax.shard_map(
        on_device, mesh=mesh, in_specs=in_specs, out_specs=out_specs, check_vma=False
    )
```

```python
import jax
import jax.numpy as jnp
from jax import lax
from jax.experimental import pallas as pl
from jax.experimental.pallas import tpu as pltpu
from jax.sharding import PartitionSpec as P

HEAD = 128
TOKENS_LOCAL = 768
FEATURES = 1024
HEAD_COLUMNS = 256
PIECE = 48
MESH = pl.DeviceIdType.MESH

beta_one = 0.9
beta_two = 0.999
correct_one = 0.19
correct_two = 0.001999
adam_eps = 1e-08
down_learning_rate = 0.003
rate_up = 0.05
adapter_scale = 2.0
rope_base = 500000.0

Z_STEPS = (1, 3, 2, 0)
X_STEPS = (2, 1, 3, 0)


def adam_step(current, moment_one, moment_two, gradient, learn_rate):
    moment_one = beta_one * moment_one + (1.0 - beta_one) * gradient
    moment_two = beta_two * moment_two + (1.0 - beta_two) * gradient * gradient
    update = moment_one / correct_one / (jnp.sqrt(moment_two / correct_two) + adam_eps)
    return (current - learn_rate * update, moment_one, moment_two)


def dot(a, b):
    return jnp.dot(a, b, preferred_element_type=jnp.float32)


def kernel(
    hidden, weight, lengths, grad_down, grad_up, p_down, m_down, v_down, p_up, m_up, v_up,
    out_h, new_down_h, new_up_h,
    hid, wv, gv, cs, cr, ys, yr, zs, zr, ab, hs, hr, hall, far, mid, near, near_b, xr, own_heads, zbs, zbr,
    table, state, up_state, up_all, out_v, new_down_v, new_up_v,
    ld_sem, core_s, core_r, y_s, y_r, z_s, z_r, a_s, a_r, f_s, f_r, hs_s, hs_r, hg_s, hg_r,
    far_s, far_r, x_s, x_r, b_s, b_r, u_s, u_r, o_sem,
):
    f = lax.axis_index("fsdp")
    t = lax.axis_index("tp")
    y, zl, c, zh, x = f // 8, (f // 2) % 4, f % 2, t // 4, t % 4
    chip = f // 2

    def f_of(y_, zl_, c_):
        return (y_ * 4 + zl_) * 2 + c_

    barrier = pltpu.get_barrier_semaphore()
    partners = [(f_of(y, zl, 1 - c), t)]
    for k in range(1, 16):
        q = (chip + k) % 16
        partners.append((q * 2 + c, t))
    for dz in range(4):
        for k in range(8):
            if k == 0:
                continue
            partners.append((f_of(y, (zl + dz) % 4, c), (t + k) % 8))
    for p in partners:
        pl.semaphore_signal(barrier, inc=1, device_id=p, device_id_type=MESH)

    heads = []
    for half in range(2):
        for dx in X_STEPS:
            zh_ = (1 - zh) if half == 0 else zh
            heads.append((half, dx, zh_ * 4 + (x + dx) % 4))
    loads = {}

    def load(name, src, dst):
        i = len(loads)
        cp = pltpu.make_async_copy(src, dst, ld_sem.at[i])
        cp.start()
        loads[name] = cp

    def load_grad(j):
        z_ = (zl + Z_STEPS[j]) % 4
        load(("d", j), grad_down.at[:, :, z_], gv.at[j, pl.ds(0, 8)])
        load(("u", j), grad_up.at[:, z_], gv.at[j, 8])

    def load_head(i):
        col = pl.multiple_of(heads[i][2] * HEAD_COLUMNS, HEAD_COLUMNS)
        load(("w", i), weight.at[:, pl.ds(col, HEAD_COLUMNS)], wv.at[i])

    load_grad(0)
    load_grad(1)
    load("hid", hidden, hid)
    load_head(0)
    load_grad(2)
    load_grad(3)
    for i in range(1, 8):
        load_head(i)
    load("p", p_down, state.at[0])
    load("m", m_down, state.at[1])
    load("v", v_down, state.at[2])
    up_state[...] = jnp.zeros_like(up_state)
    load("pu", p_up, up_state.at[pl.ds(0, 4)])
    load("mu", m_up, up_state.at[pl.ds(8, 4)])
    load("vu", v_up, up_state.at[pl.ds(16, 4)])

    def send(src, dst, ss, rs, to):
        pltpu.make_async_remote_copy(
            src_ref=src, dst_ref=dst, send_sem=ss, recv_sem=rs, device_id=to, device_id_type=MESH
        ).start()

    def await_bytes(ref, sem):
        pltpu.make_async_copy(ref, ref, sem).wait()

    sent = []

    def phase_a(j):
        loads[("d", j)].wait()
        loads[("u", j)].wait()

        @pl.loop(0, 4)
        def _(k):
            cs[j, k] = gv[j, :, (y + k) % 4, 1 - c].astype(jnp.bfloat16)

    def core_send(j):
        send(cs.at[j], cr.at[j], core_s.at[j], core_r.at[j], (f_of(y, zl, 1 - c), t))
        sent.append((cs.at[j], core_s.at[j]))

    def phase_b(j):
        await_bytes(cr.at[j], core_r.at[j])
        for k in (2, 1, 3):
            ys[j, k - 1] = (
                gv[j, :, (y + k) % 4, c] + cr[j, k].astype(jnp.float32)
            ).astype(jnp.bfloat16)
            send(
                ys.at[j, k - 1], yr.at[j, k - 1], y_s.at[j, k - 1], y_r.at[j, k - 1],
                (f_of((y + k) % 4, zl, c), t),
            )
            sent.append((ys.at[j, k - 1], y_s.at[j, k - 1]))

    rows = lax.broadcasted_iota(jnp.int32, (128, 32), 0)
    cols = lax.broadcasted_iota(jnp.int32, (128, 32), 1)
    tile, r = rows // 16, rows % 16
    wanted = jnp.where(
        r < 4, 4 * tile + r, jnp.where(r < 6, 2 * tile + r - 4, 2 * tile + r + 10)
    )
    pick = jnp.where((wanted == cols) & (r < 8), 1.0, 0.0).astype(jnp.bfloat16)

    def phase_c(j):
        for k in range(3):
            await_bytes(yr.at[j, k], y_r.at[j, k])
        total = (
            gv[j, :, y, c]
            + cr[j, 0].astype(jnp.float32)
            + yr[j, 0].astype(jnp.float32)
            + yr[j, 1].astype(jnp.float32)
            + yr[j, 2].astype(jnp.float32)
        ).astype(jnp.bfloat16)
        zs[j, :, 0:32] = total[0:8]
        zs[j, :, 32:48] = dot(pick, total[8]).astype(jnp.bfloat16).reshape(8, 16, 128)
        to_f = f_of(y, (zl + Z_STEPS[j]) % 4, c)
        for k in range(8):
            if Z_STEPS[j] == 0 and k == 0:
                continue
            to_t = (t + k) % 8
            send(zs.at[j, to_t], zr.at[j, k], z_s.at[j], z_r.at[j], (to_f, to_t))
        sent.append((zs.at[j] if Z_STEPS[j] else zs.at[j, pl.ds(1, 7)], z_s.at[j]))

    def up_exchange():
        for name in ("pu", "mu", "vu"):
            loads[name].wait()
        up_all[t] = up_state[...]
        for k in range(1, 8):
            send(up_state, up_all.at[t], u_s, u_r, (f, (t + k) % 8))
        sent.append((up_all.at[pl.ds(0, 7)], u_s))

    upper, lower = pl.ds(0, 384), pl.ds(384, 384)
    x_next, x_prev = (f, zh * 4 + (x + 1) % 4), (f, zh * 4 + (x + 3) % 4)

    def product(i, place):
        loads[("w", i)].wait()

        @pl.loop(0, 3)
        def _(m):
            part = pl.ds(pl.multiple_of(m * 256, 256), 256)
            place[part, :] = dot(hid[part, :], wv[i]).astype(place.dtype)

    def far_head(half):
        product(half * 4, far.at[half])

    def far_send(half):
        send(far.at[half, upper], mid.at[half, 0], far_s.at[half, 0], far_r.at[half, 0], x_next)
        send(far.at[half, lower], mid.at[half, 1], far_s.at[half, 1], far_r.at[half, 1], x_prev)
        sent.append((far.at[half, upper], far_s.at[half, 0]))
        sent.append((far.at[half, lower], far_s.at[half, 1]))

    def near_head(half, side):
        product(half * 4 + 1 + side, near.at[side])
        mine = lower if side == 0 else upper

        @pl.loop(0, 3)
        def _(m):
            part = pl.ds(pl.multiple_of((384 if side == 0 else 0) + m * 128, 128), 128)
            near_b[half, side, part, :] = near[side, part, :].astype(jnp.bfloat16)

        send(
            near_b.at[half, side, mine], xr.at[half, side, mine], x_s.at[half, side, 0], x_r.at[half, side, 0],
            x_next if side == 0 else x_prev,
        )
        sent.append((near_b.at[half, side, mine], x_s.at[half, side, 0]))

    def near_sum(half, side):
        await_bytes(mid.at[half, side], far_r.at[half, side])
        mine = upper if side == 0 else lower

        @pl.loop(0, 3)
        def _(m):
            local = pl.ds(pl.multiple_of(m * 128, 128), 128)
            part = pl.ds(pl.multiple_of((0 if side == 0 else 384) + m * 128, 128), 128)
            near_b[half, side, part, :] = (
                near[side, part, :] + mid[half, side, local, :].astype(jnp.float32)
            ).astype(jnp.bfloat16)

        send(
            near_b.at[half, side, mine], xr.at[half, side, mine], x_s.at[half, side, 1], x_r.at[half, side, 1],
            x_next if side == 0 else x_prev,
        )
        sent.append((near_b.at[half, side, mine], x_s.at[half, side, 1]))

    def own_head(half):
        product(half * 4 + 3, own_heads.at[half])

    def head_arrive(half):
        for side in range(2):
            await_bytes(xr.at[half, side, lower], x_r.at[half, side, 0])
            await_bytes(xr.at[half, side, upper], x_r.at[half, side, 1])

    def head_forward(h):
        if h == 0:
            head_arrive(0)

        @pl.loop(3 * h, 3 * h + 3)
        def _(m):
            part = pl.ds(pl.multiple_of(m * 128, 128), 128)
            zbs[part, :] = (
                own_heads[0, part, :]
                + xr[0, 0, part, :].astype(jnp.float32)
                + xr[0, 1, part, :].astype(jnp.float32)
            ).astype(jnp.bfloat16)

        half_part = pl.ds(384 * h, 384)
        send(zbs.at[half_part], zbr.at[half_part], b_s.at[h], b_r.at[h], (f, (1 - zh) * 4 + x))
        sent.append((zbs.at[half_part], b_s.at[h]))

    def trig():
        lane = lax.broadcasted_iota(jnp.int32, (128, 128), 1)
        freq = jnp.exp(
            (lane % 64).astype(jnp.float32) * (-2.0 / HEAD * 13.122363377404328)
        )
        shift = jnp.where(lane < 64, 0.5 * 3.141592653589793, 0.0)

        @pl.loop(0, 6)
        def _(m):
            index = lax.broadcasted_iota(jnp.int32, (128, 128), 0) + m * 128
            start = jnp.zeros((128, 128), jnp.int32)
            end = jnp.int32(0)
            for d in range(6):
                end = end + lengths[0, d]
                start = start + jnp.where(index >= end, lengths[0, d], 0)
            angle = (index - start).astype(jnp.float32) * freq
            table[pl.ds(pl.multiple_of(m * 128, 128), 128), :] = jnp.sin(angle + shift)

    phase_a(0)
    phase_a(1)
    loads["hid"].wait()
    far_head(0)
    phase_a(2)
    phase_a(3)
    pl.semaphore_wait(barrier, len(partners))
    for j in range(4):
        core_send(j)
    far_send(0)
    phase_b(0)
    near_head(0, 0)
    phase_b(1)
    near_head(0, 1)
    phase_b(2)
    phase_b(3)
    up_exchange()
    near_sum(0, 0)
    near_sum(0, 1)
    phase_c(0)
    own_head(0)
    phase_c(1)
    far_head(1)
    phase_c(2)
    phase_c(3)
    far_send(1)
    near_head(1, 0)
    near_head(1, 1)
    own_head(1)
    trig()
    select_row = lax.broadcasted_iota(jnp.int32, (128, 512), 0)
    select_col = lax.broadcasted_iota(jnp.int32, (128, 512), 1)
    place = (select_row % 64) // 2 * 16 + select_row % 2 * 2
    key_pick = jnp.where((select_row < 64) & (select_col == place), 1.0, 0.0)
    value_pick = jnp.where((select_row >= 64) & (select_col == place + 1), 1.0, 0.0)
    head_forward(0)
    for j in range(3):
        await_bytes(zr.at[j], z_r.at[j])
    await_bytes(zr.at[3, pl.ds(1, 7)], z_r.at[3])
    total = zs[3, t].astype(jnp.float32)
    for j in range(4):
        for k in range(8):
            if j == 3 and k == 0:
                continue
            total = total + zr[j, k].astype(jnp.float32)
    for name in ("p", "m", "v"):
        loads[name].wait()
    new = adam_step(state[0], state[1], state[2], total[0:32], down_learning_rate)
    ab[chip, c, 0:32] = new[0].astype(jnp.bfloat16)
    await_bytes(up_all.at[pl.ds(0, 7)], u_r)
    first, second = up_all[t // 2], up_all[4 + t // 2]
    odd = t % 2 == 1

    def of_head(row):
        return jnp.concatenate(
            [
                jnp.where(odd, first[row + 2 : row + 4], first[row : row + 2]),
                jnp.where(odd, second[row + 2 : row + 4], second[row : row + 2]),
            ],
            axis=0,
        )

    new_head = adam_step(of_head(0), of_head(8), of_head(16), total[36:40], rate_up)[0]
    ab[chip, c, 32:48] = jnp.concatenate(
        [new_head, jnp.zeros((12, 128), jnp.float32)], axis=0
    ).astype(jnp.bfloat16)
    for k in range(1, 16):
        q = (chip + k) % 16
        send(ab.at[chip, c], ab.at[chip, c], a_s, a_r, (q * 2 + c, t))
    sent.append((ab.at[pl.ds(0, 15), c], a_s))
    new_up = adam_step(
        up_state[0:4], up_state[8:12], up_state[16:20], total[32:36], rate_up
    )
    for n in range(3):
        new_down_v[n] = new[n]
        new_up_v[n] = jnp.concatenate([new_up[n], new_up[n]], axis=0)
    outs = [
        pltpu.make_async_copy(new_down_v, new_down_h, o_sem.at[0]),
        pltpu.make_async_copy(new_up_v, new_up_h, o_sem.at[1]),
    ]
    for move in outs:
        move.start()

    near_sum(1, 0)
    near_sum(1, 1)
    await_bytes(ab.at[pl.ds(0, 15), c], a_r)
    send(ab.at[:, c], ab.at[:, c], f_s, f_r, (f_of(y, zl, 1 - c), t))
    sent.append((ab.at[:, c], f_s))
    await_bytes(ab.at[:, 1 - c], f_r)

    adapter = ab[:, :, 0:32].reshape(FEATURES, 128)
    for m in range(2):
        part = pl.ds(m * 384, 384)
        hs[m * 4 : m * 4 + 4] = dot(hid[part, :], adapter).astype(jnp.bfloat16).reshape(4, 96, 128)
    for k in range(1, 8):
        to_t = (t + k) % 8
        send(hs.at[to_t], hr.at[k - 1], hs_s, hs_r, (f, to_t))
    sent.append((hr, hs_s))
    rolls = ab[:, :, 32:48].reshape(512, 128)
    key_block = dot(key_pick.astype(jnp.bfloat16), rolls).astype(jnp.bfloat16)
    value_block = dot(value_pick.astype(jnp.bfloat16), rolls).astype(jnp.bfloat16)

    head_forward(1)
    await_bytes(hr, hs_r)
    mixed = hs[t].astype(jnp.float32)
    for k in range(7):
        mixed = mixed + hr[k].astype(jnp.float32)
    hall[t] = mixed.astype(jnp.bfloat16)
    for k in range(1, 8):
        send(hall.at[t], hall.at[t], hg_s, hg_r, (f, (t + k) % 8))
    sent.append((hr, hg_s))

    head_arrive(1)
    await_bytes(zbr.at[pl.ds(0, 384)], b_r.at[0])
    await_bytes(zbr.at[pl.ds(384, 384)], b_r.at[1])

    @pl.loop(0, 6)
    def _(m):
        part = pl.ds(pl.multiple_of(m * 128, 128), 128)
        own_heads[1, part, :] = (
            own_heads[1, part, :]
            + xr[1, 0, part, :].astype(jnp.float32)
            + xr[1, 1, part, :].astype(jnp.float32)
            + zbr[part, :].astype(jnp.float32)
        )

    await_bytes(hall.at[pl.ds(0, 7)], hg_r)
    low = lax.broadcasted_iota(jnp.int32, (96, 128), 1) < 64
    for m in range(8):
        part = pl.ds(m * 96, 96)
        if m == 4:
            half_rows = pl.ds(0, 384)
            outs.append(pltpu.make_async_copy(out_v.at[half_rows], out_h.at[half_rows], o_sem.at[2]))
            outs[-1].start()
        rot = table[part, :]
        swapped = pltpu.roll(rot, 64, 1)
        cosine = jnp.where(low, rot, swapped)
        sine = jnp.where(low, -swapped, rot)
        key = own_heads[1, part, 0:128] + adapter_scale * dot(hall[m], key_block)
        value = own_heads[1, part, 128:256] + adapter_scale * dot(hall[m], value_block)
        out_v[part, 0:128] = (key * cosine + pltpu.roll(key, 64, 1) * sine).astype(jnp.bfloat16)
        out_v[part, 128:256] = value.astype(jnp.bfloat16)

    half_rows = pl.ds(384, 384)
    outs.append(pltpu.make_async_copy(out_v.at[half_rows], out_h.at[half_rows], o_sem.at[3]))
    outs[-1].start()

    for ref, sem in sent:
        await_bytes(ref, sem)
    for move in outs:
        move.wait()


def write_out(states, down, up, *refs):
    outs, sem = refs[:7], refs[7]
    parts = [states] + [down.at[n] for n in range(3)] + [up.at[n, pl.ds(0, 4)] for n in range(3)]
    moves = [pltpu.make_async_copy(a, b, sem.at[n]) for n, (a, b) in enumerate(zip(parts, outs))]
    for move in moves:
        move.start()
    for move in moves:
        move.wait()


def on_device(
    hidden_states, key_value_weight, doc_lengths, grad_down, grad_up,
    adapter_down, first_down, second_down, adapter_up, first_up, second_up,
):
    bf16, f32 = jnp.bfloat16, jnp.float32
    anywhere = pl.BlockSpec(memory_space=pl.ANY)
    vm = pltpu.VMEM
    dma = pltpu.SemaphoreType.DMA
    results = pl.pallas_call(
        kernel,
        out_shape=[
            jax.ShapeDtypeStruct((TOKENS_LOCAL, HEAD_COLUMNS), bf16),
            jax.ShapeDtypeStruct((3, 32, 128), f32),
            jax.ShapeDtypeStruct((3, 8, 128), f32),
        ],
        in_specs=[anywhere, anywhere, pl.BlockSpec(memory_space=pltpu.SMEM)] + [anywhere] * 8,
        out_specs=[anywhere] * 3,
        scratch_shapes=[
            vm((TOKENS_LOCAL, FEATURES), bf16),
            vm((8, FEATURES, HEAD_COLUMNS), bf16),
            vm((4, 9, 4, 2, 32, 128), f32),
            vm((4, 4, 9, 32, 128), bf16),
            vm((4, 4, 9, 32, 128), bf16),
            vm((4, 3, 9, 32, 128), bf16),
            vm((4, 3, 9, 32, 128), bf16),
            vm((4, 8, PIECE, 128), bf16),
            vm((4, 8, PIECE, 128), bf16),
            vm((16, 2, PIECE, 128), bf16),
            vm((8, 96, 128), bf16),
            vm((7, 96, 128), bf16),
            vm((8, 96, 128), bf16),
            vm((2, TOKENS_LOCAL, HEAD_COLUMNS), bf16),
            vm((2, 2, TOKENS_LOCAL // 2, HEAD_COLUMNS), bf16),
            vm((2, TOKENS_LOCAL, HEAD_COLUMNS), f32),
            vm((2, 2, TOKENS_LOCAL, HEAD_COLUMNS), bf16),
            vm((2, 2, TOKENS_LOCAL, HEAD_COLUMNS), bf16),
            vm((2, TOKENS_LOCAL, HEAD_COLUMNS), f32),
            vm((TOKENS_LOCAL, HEAD_COLUMNS), bf16),
            vm((TOKENS_LOCAL, HEAD_COLUMNS), bf16),
            vm((TOKENS_LOCAL, 128), f32),
            vm((3, 32, 128), f32),
            vm((24, 128), f32),
            vm((8, 24, 128), f32),
            vm((TOKENS_LOCAL, HEAD_COLUMNS), bf16),
            vm((3, 32, 128), f32),
            vm((3, 8, 128), f32),
            dma((24,)),
            dma((4,)), dma((4,)),
            dma((4, 3)), dma((4, 3)),
            dma((4,)), dma((4,)),
            dma(()), dma(()),
            dma(()), dma(()),
            dma(()), dma(()),
            dma(()), dma(()),
            dma((2, 2)), dma((2, 2)),
            dma((2, 2, 2)), dma((2, 2, 2)),
            dma((2,)), dma((2,)),
            dma(()), dma(()),
            dma((4,)),
        ],
        compiler_params=pltpu.CompilerParams(
            collective_id=0, has_side_effects=True, vmem_limit_bytes=56 * 1024 * 1024
        ),
        cost_estimate=pl.CostEstimate(
            flops=2 * TOKENS_LOCAL * FEATURES * 2200, bytes_accessed=12 << 20, transcendentals=0
        ),
    )(
        hidden_states,
        key_value_weight,
        doc_lengths,
        grad_down.reshape(8, 4, 4, 2, 32, 128),
        grad_up.reshape(4, 4, 2, 32, 128),
        adapter_down[0],
        first_down[0],
        second_down[0],
        adapter_up,
        first_up,
        second_up,
    )
    states, p_down, m_down, v_down, p_up, m_up, v_up = pl.pallas_call(
        write_out,
        out_shape=[jax.ShapeDtypeStruct((TOKENS_LOCAL, HEAD_COLUMNS), bf16)]
        + [jax.ShapeDtypeStruct((32, 128), f32)] * 3
        + [jax.ShapeDtypeStruct((4, 128), f32)] * 3,
        in_specs=[pl.BlockSpec(memory_space=vm)] * 3,
        out_specs=[anywhere] * 7,
        scratch_shapes=[dma((7,))],
    )(*results)
    return (states, p_down[None], m_down[None], v_down[None], p_up, m_up, v_up)


def solution(mesh):
    matrix = P(("fsdp", "tp"), None)
    down = P("tp", "fsdp", None)
    partial = P(("fsdp", "tp"), None, None)
    in_specs = (
        P("fsdp", "tp"), P("tp", None), P("fsdp", None), partial, partial,
        down, down, down, matrix, matrix, matrix,
    )
    out_specs = (P("fsdp", "tp"), down, down, down, matrix, matrix, matrix)
    return jax.shard_map(
        on_device, mesh=mesh, in_specs=in_specs, out_specs=out_specs, check_vma=False
    )
```
